32 devices in a mesh: dom: 4 (over y, core), row: 4 (over z), col: 2 (over x).
Axes of the slice: x: 2, y: 2, z: 4, core: 2. Of those that a mesh axis runs over, the one named last changes fastest.
Arguments:
- phi: bfloat16 [64, 2048, 256], P('dom', None, 'col'), may hold values from -0.125 to 0.125
- couple_k: bfloat16 [64, 2048, 2, 512], P('dom', None, None, 'row'), may hold values from -1.1953125 to 1.1953125
- couple_m: bfloat16 [64, 2048, 2, 512], P('dom', None, None, 'row'), may hold values from -1.1953125 to 1.1953125
- eigen: float32 [64, 256], P('dom', 'col'), may hold values from 1 to 16
- sizes: int32 [64], P('dom'), may hold values from 1 to 2048, 98304 in all
- adjacency: int32 [64, 2], P('dom'), may hold values from 0 to 3, all different within a row
- k_bb: float32 [4, 512, 512], P('dom', 'row', 'col'), may hold values from -6 to 6
- m_bb: float32 [4, 512, 512], P('dom', 'row', 'col'), may hold values from -6 to 6
Outputs:
- k_red: float32 [4, 512, 512], P('dom', 'row', 'col')
- m_red: float32 [4, 512, 512], P('dom', 'row', 'col')
The draws below stay inside these ranges and needn't reach their ends.
Inputs may be any that keep to these rules, and one draw needn't show every extreme that they name: `adjacency`: the two separators of a substructure differ, and every separator is touched by some substructure.
All inputs are finite; a program needn't handle non-finite values. No bound on the sum of `sizes` on one device may be relied on, other than what follows from the above.
Results may differ from the reference program's by a relative error of at most 0.0035.
Values may be sent and summed in bfloat16 or wider, within the bound.
A program may use at most 192 MiB of HBM per device.

```python
import math
import jax
import jax.numpy as jnp
import numpy as np
from jax import lax

NI = 2048
P_SIZE = 256
NB = 512
SUBS = 64
NSEP = 4


def block_levels(own_key, extent, pieces, low, largest):
    factor_of, own = 1.0, jax.random.fold_in(own_key, 6)
    for position, parts in pieces:
        steps = jnp.exp(jax.random.uniform(jax.random.fold_in(own, position), (parts,), jnp.float32, low / len(pieces), largest / len(pieces)))
        factor_of = factor_of * jnp.repeat(steps, extent[position] // parts).reshape([-1 if axis == position else 1 for axis in range(len(extent))])
    return factor_of


def distinct(rng, rows, number_of, top, lift):
    sequence = jax.random.permutation(jax.random.fold_in(rng, 1), number_of)
    favour = sequence
    for power in range(3):
        favour = favour * favour // number_of
    favour = favour * lift // number_of
    chance = jax.random.randint(jax.random.fold_in(rng, 2), (rows, number_of), 0, 4096) + favour
    fixed_rows = jax.random.permutation(jax.random.fold_in(rng, 3), rows)[jnp.arange(number_of) % rows]
    chance = jnp.where(jnp.arange(rows)[:, None] == fixed_rows[None, :], 1 << 14, chance)
    priority = chance * number_of + jnp.arange(number_of)
    return lax.top_k(priority.astype(jnp.int32), top)[1].astype(jnp.int32)


def profile(count, total, bound, skew):
    portions = [(1 << 20) // math.isqrt(standing ** skew) + 1 for standing in range(2, count + 1)]
    rest, counts = total - bound - (count - 1), [1] * (count - 1)
    while rest > 0:
        candidates = [i for i in range(count - 1) if counts[i] < bound]
        whole, left = sum([portions[i] for i in candidates]), rest
        for i in candidates:
            extra = min(bound - counts[i], max(1, left * portions[i] // whole), rest)
            counts[i] = counts[i] + extra
            rest = rest - extra
    return np.array([bound] + counts)


def uneven(key, number_of, total, reach, skew):
    if number_of == 2:
        one = jax.random.randint(key, (), max(1, total - reach), min(reach, total - 1) + 1)
        return jnp.stack([one, total - one])
    tallies = jnp.asarray(profile(number_of, total, reach, skew), jnp.int32)
    couples = (number_of - 1) // 2
    source_of, receiver = tallies[1:1 + 2 * couples:2], tallies[2:2 + 2 * couples:2]
    room = jnp.minimum(source_of - 1, reach - receiver)
    passed = jax.random.randint(jax.random.fold_in(key, 1), (couples,), 0, 1 << 20) % (room + 1)
    tallies = tallies.at[1:1 + 2 * couples:2].set(source_of - passed).at[2:2 + 2 * couples:2].set(receiver + passed)
    return tallies[jax.random.permutation(jax.random.fold_in(key, 2), number_of)]


def centred(stream_key, extent, width, limit, shards=(), kind=jnp.bfloat16):
    entries = jax.random.normal(stream_key, extent, jnp.float32) * width
    if len(shards) > 0:
        entries = block_levels(stream_key, extent, shards, -0.22, 0.18) * entries
    return jnp.clip(entries, min=-limit, max=limit).astype(kind)


def setup_inputs(seed: int = 0) -> dict:
    streams_of = jax.random.split(jax.random.key(seed), 9)
    phi = centred(streams_of[0], (SUBS, NI, P_SIZE), NI ** -0.5, 0.125, ((0, 4), (2, 2)))
    couple_k = centred(streams_of[1], (SUBS, NI, 2, NB), 0.2, 1.1953125, ((0, 4), (3, 4)))
    couple_m = centred(streams_of[2], (SUBS, NI, 2, NB), 0.2, 1.1953125, ((0, 4), (3, 4)))
    eigen = jnp.clip(jnp.exp(math.log(16.0) - 2.7725887 * jax.random.uniform(streams_of[3], (SUBS, P_SIZE), jnp.float32) ** block_levels(streams_of[3], (SUBS, P_SIZE), ((0, 4), (1, 2)), -0.2, 0.2)), 1.0, 16.0)
    sizes = uneven(streams_of[4], SUBS, 3 * SUBS * NI // 4, NI, 2).astype(jnp.int32)
    adjacency = distinct(streams_of[5], SUBS, NSEP, 2, 8192)
    k_bb = centred(streams_of[6], (NSEP, NB, NB), 1.0, 6.0, ((0, 4), (1, 4), (2, 2)), jnp.float32)
    m_bb = centred(streams_of[7], (NSEP, NB, NB), 1.0, 6.0, ((0, 4), (1, 4), (2, 2)), jnp.float32)
    return {"phi": phi, "couple_k": couple_k, "couple_m": couple_m, "eigen": eigen, "sizes": sizes, "adjacency": adjacency, "k_bb": k_bb, "m_bb": m_bb}


def reference(phi, couple_k, couple_m, eigen, sizes, adjacency, k_bb, m_bb):
    def project(items):
        phi_s, stiff_s, mass_s, size = items
        rows = jnp.arange(NI, dtype=jnp.int32)[:, None]
        masked = jnp.where(rows < size, phi_s, jnp.zeros_like(phi_s))
        coeff_k = jnp.dot(masked.T, stiff_s.reshape(NI, 2 * NB), preferred_element_type=jnp.float32)
        coeff_m = jnp.dot(masked.T, mass_s.reshape(NI, 2 * NB), preferred_element_type=jnp.float32)
        coeff_k = coeff_k.astype(jnp.bfloat16).reshape(P_SIZE, 2, NB)
        coeff_m = coeff_m.astype(jnp.bfloat16).reshape(P_SIZE, 2, NB)
        return jnp.transpose(coeff_k, (1, 0, 2)), jnp.transpose(coeff_m, (1, 0, 2))

    coeff_k, coeff_m = lax.map(project, (phi, couple_k, couple_m, sizes))
    coeff_k = coeff_k.reshape(SUBS * 2, P_SIZE, NB)
    coeff_m = coeff_m.reshape(SUBS * 2, P_SIZE, NB)
    values = jnp.repeat(eigen, 2, axis=0)
    targets = adjacency.reshape(SUBS * 2).astype(jnp.int32)

    def accumulate(carry, items):
        acc_k, acc_m = carry
        stiff, mass, lam, target = items
        lam = lam[:, None]
        scaled_k = (stiff.astype(jnp.float32) / lam).astype(jnp.bfloat16)
        scaled_m = (mass.astype(jnp.float32) / lam).astype(jnp.bfloat16)
        scaled_kk = (stiff.astype(jnp.float32) / (lam * lam)).astype(jnp.bfloat16)
        corr_k = -jnp.dot(scaled_k.T, stiff, preferred_element_type=jnp.float32)
        corr_m = -(jnp.dot(scaled_k.T, mass, preferred_element_type=jnp.float32)
                   + jnp.dot(scaled_m.T, stiff, preferred_element_type=jnp.float32))
        corr_m = corr_m + jnp.dot(scaled_kk.T, stiff, preferred_element_type=jnp.float32)
        return (acc_k.at[target].add(corr_k), acc_m.at[target].add(corr_m)), None

    start = (jnp.zeros((NSEP, NB, NB), jnp.float32), jnp.zeros((NSEP, NB, NB), jnp.float32))
    (acc_k, acc_m), _ = lax.scan(accumulate, start, (coeff_k, coeff_m, values, targets))
    return k_bb + acc_k, m_bb + acc_m
```

```python
import functools

import jax
import jax.numpy as jnp
from jax import lax
from jax.experimental import pallas as pl
from jax.experimental.pallas import tpu as pltpu
from jax.sharding import PartitionSpec as P

MESH = pl.DeviceIdType.MESH
BF = jnp.bfloat16
F32 = jnp.float32


def kernel(dims, sizes_ref, phi_ref, ck_ref, cm_ref, lam_ref, sel_ref, out_ref,
           pbuf, kbuf, mbuf, rep, stage, coef_k, coef_m, sk_t, w_t, sk_r, w_r, part, last, *rest):
    nsub, ni, np_, nb, nrow, ncol, nsep, nbits, plans = dims
    nrecv = sum(len(p) for p in plans)
    recvs = rest[:nrecv]
    (load_sem, send_sem, recv_sem, red_send, red_recv, last_send, last_recv) = rest[nrecv:]
    dom, row, col = lax.axis_index("dom"), lax.axis_index("row"), lax.axis_index("col")
    groups = nsub // nrow
    wide = nb * nrow
    half = wide // ncol

    def partner(step):
        if step == "col":
            return (dom, row, 1 - col)
        bit = (dom // (1 << step)) % 2
        return (dom + (1 - 2 * bit) * (1 << step), row, col)

    def peer(k):
        return (dom, lax.rem(row + k, nrow), col)

    def loads(t, slot):
        s = (t // nrow) * nrow + lax.rem(row + 1 + lax.rem(t, nrow), nrow)
        return [
            pltpu.make_async_copy(phi_ref.at[s], pbuf.at[slot], load_sem.at[slot, 0]),
            pltpu.make_async_copy(ck_ref.at[s], kbuf.at[slot], load_sem.at[slot, 1]),
            pltpu.make_async_copy(cm_ref.at[s], mbuf.at[slot], load_sem.at[slot, 2]),
        ]

    for c in loads(0, 0):
        c.start()

    barrier = pltpu.get_barrier_semaphore()
    others = [peer(k) for k in range(1, nrow)] + [partner(b) for b in range(nbits)] + [partner("col")]
    for other in others:
        pl.semaphore_signal(barrier, inc=1, device_id=other, device_id_type=MESH)
    pl.semaphore_wait(barrier, len(others))

    chunk = 512
    lanes = lax.broadcasted_iota(jnp.int32, (1, 2 * chunk), 1) % 2
    even = (1 - lanes).astype(F32).astype(BF)
    odd = lanes.astype(F32).astype(BF)
    mine = pl.ds(pl.multiple_of(row * nb, 128), nb)

    def project(i, k, slot):
        t = i * nrow + k
        s = i * nrow + lax.rem(row + 1 + k, nrow)
        nxt = t + 1

        @pl.when(nxt < nsub)
        def _():
            for c in loads(nxt, 1 - slot):
                c.start()

        for c in loads(t, slot):
            c.wait()
        size = sizes_ref[s]

        def piece(h, acc):
            base = pl.multiple_of(h * chunk, chunk)
            rows = lax.broadcasted_iota(jnp.int32, (chunk, np_), 0) + base
            ph = pbuf[slot, pl.ds(base, chunk), :].astype(F32)
            ph = jnp.where(rows < size, ph, 0.0)
            rep[pl.ds(0, chunk, stride=2), :] = ph
            rep[pl.ds(1, chunk, stride=2), :] = ph
            rt = rep[...].astype(BF).T
            left = jnp.concatenate([rt * even, rt * odd], axis=0)
            base2 = pl.multiple_of(h * 2 * chunk, 2 * chunk)
            right = jnp.concatenate(
                [kbuf[slot, pl.ds(base2, 2 * chunk), :], mbuf[slot, pl.ds(base2, 2 * chunk), :]], axis=1
            )
            return acc + jnp.dot(left, right, preferred_element_type=F32)

        acc = lax.fori_loop(0, ni // chunk, piece, jnp.zeros((2 * np_, 2 * nb), F32))
        return acc.astype(BF)

    def sends(i, k):
        return [
            pltpu.make_async_remote_copy(
                src_ref=stage.at[i, k, q], dst_ref=dst.at[i, :, mine],
                send_sem=send_sem.at[i, k, q], recv_sem=recv_sem.at[i, k, q],
                device_id=peer(k + 1), device_id_type=MESH,
            )
            for q, dst in ((0, coef_k), (1, coef_m))
        ]

    def group(i, _):
        for k in range(nrow):
            val = project(i, k, k % 2)
            if k < nrow - 1:
                stage[i, k, 0] = val[:, :nb]
                stage[i, k, 1] = val[:, nb:]
                for c in sends(i, k):
                    c.start()
            else:
                coef_k[i, :, mine] = val[:, :nb]
                coef_m[i, :, mine] = val[:, nb:]
        return 0

    lax.fori_loop(0, groups, group, 0)

    for i in range(groups):
        for k in range(nrow - 1):
            for c in sends(i, k):
                c.wait()
        s = i * nrow + row
        for j in range(2):
            rows = slice(j * np_, (j + 1) * np_)
            at = (i * 2 + j) * np_
            inv = 1.0 / lam_ref[s]
            inv = jnp.concatenate([inv] * (wide // 128), axis=1)
            ck = coef_k[i, rows, :].astype(F32)
            cm = coef_m[i, rows, :].astype(F32)
            sk = ck * inv
            w = cm - 0.5 * sk
            sk_r[at:at + np_, :] = sk.astype(BF)
            w_r[at:at + np_, :] = w.astype(BF)
            sk_t[:, at:at + np_] = sk.T.astype(BF)
            w_t[:, at:at + np_] = w.T.astype(BF)

    depth = groups * 2 * np_

    def gram(q, e):
        sel = sel_ref[row, pl.ds(e, 1), :].astype(BF)
        for a in range(0, wide, 256):
            lhs = sk_t[a:a + 256, :] * sel
            if q == 0:
                val = jnp.dot(lhs, flat_k(), preferred_element_type=F32)
            else:
                val = jnp.dot(lhs, w_r[...], preferred_element_type=F32)
                val += jnp.dot(w_t[a:a + 256, :] * sel, sk_r[...], preferred_element_type=F32)
            part[q, e // 2, e % 2, a:a + 256, :] = (-val).astype(BF)

    def flat_k():
        return coef_k[...].reshape(depth, wide)

    def exchange(q, n):
        step = plans[q][n]
        at = sum(len(p) for p in plans[:q]) + n
        src = part.at[q] if n == 0 else recvs[at - 1]
        return step, at, src

    def rcopy(q, n):
        step, at, src = exchange(q, n)
        if step == "col":
            send = src.at[:, :, :, pl.ds(pl.multiple_of((1 - col) * half, 128), half)]
        else:
            bit = (dom // (1 << step)) % 2
            send = src.at[:, 1 - bit]
        dst = recvs[at]
        if step != "col":
            dst = merged(dst)
        return pltpu.make_async_remote_copy(
            src_ref=send, dst_ref=dst, send_sem=red_send.at[at], recv_sem=red_recv.at[at],
            device_id=partner(step), device_id_type=MESH,
        )

    def merged(ref):
        a, b, r, c = ref.shape
        return ref.reshape(a * b, r, c)

    def combine(q, n):
        step, at, src = exchange(q, n)
        dst = recvs[at]
        a, b, r, c = dst.shape
        for x in range(a):
            for y in range(b):
                if step == "col":
                    own = src.at[x, y, :, pl.ds(pl.multiple_of(col * half, 128), half)]
                else:
                    own = src.at[x * b + y, (dom // (1 << step)) % 2]

                @pl.loop(0, r // 128)
                def _(z):
                    rs = pl.ds(pl.multiple_of(z * 128, 128), 128)
                    dst[x, y, rs, :] = (dst[x, y, rs, :].astype(F32) + own[rs, :].astype(F32)).astype(BF)

    for q in range(2):
        @pl.loop(0, nsep)
        def _(e):
            gram(q, e)
        rcopy(q, 0).start()

    for n in range(len(plans[0])):
        for q in range(2):
            rcopy(q, n).wait_recv()
            combine(q, n)
            if n + 1 < len(plans[q]):
                rcopy(q, n + 1).start()
            else:
                for k in range(1, nrow):
                    lcopy(q, k, recvs, plans, last, last_send, last_recv, peer, nb, row, nrow).start()
    for q in range(2):
        fin = recvs[sum(len(p) for p in plans[:q + 1]) - 1]
        total = fin[0, 0, mine, :].astype(F32)
        for k in range(1, nrow):
            lcopy(q, k, recvs, plans, last, last_send, last_recv, peer, nb, row, nrow).wait()
            total += last[q, k - 1].astype(F32)
        out_ref[q] = total
        for n in range(len(plans[q])):
            rcopy(q, n).wait_send()


def lcopy(q, k, recvs, plans, last, last_send, last_recv, peer, nb, row, nrow):
    fin = recvs[sum(len(p) for p in plans[:q + 1]) - 1]
    to = lax.rem(row + k, nrow)
    return pltpu.make_async_remote_copy(
        src_ref=fin.at[0, 0, pl.ds(pl.multiple_of(to * nb, 128), nb), :],
        dst_ref=last.at[q, k - 1],
        send_sem=last_send.at[q, k - 1], recv_sem=last_recv.at[q, k - 1],
        device_id=peer(k), device_id_type=MESH,
    )


def per_device(phi, couple_k, couple_m, eigen, sizes, adjacency, k_bb, m_bb):
    nsub, ni, np_ = phi.shape
    nb = couple_k.shape[3]
    nrow, ncol, nsep = lax.axis_size("row"), lax.axis_size("col"), lax.axis_size("dom")
    nbits = nsep.bit_length() - 1
    wide = nb * nrow
    half = wide // ncol
    groups = nsub // nrow
    ck = couple_k.reshape(nsub, 2 * ni, nb)
    cm = couple_m.reshape(nsub, 2 * ni, nb)
    lam = jnp.broadcast_to(eigen[:, :, None], (nsub, np_, 128))
    sel = (adjacency[None] == lax.broadcasted_iota(jnp.int32, (nsep, 1, 1), 0)).astype(F32)
    sel = sel.reshape(nsep, groups, nrow, 2).transpose(2, 0, 1, 3)
    sel = jnp.repeat(sel.reshape(nrow, nsep, groups * 2), np_, axis=2)
    plans = (tuple(range(nbits)) + ("col",), (0, "col") + tuple(range(1, nbits)))
    recvs = []
    for plan in plans:
        count, width = nsep, wide
        for n, step in enumerate(plan):
            if step == "col":
                width = half
            else:
                count //= 2
            later = [x for x in plan[n + 1:] if x != "col"]
            shape = (count // 2, 2, wide, width) if later else (1, 1, wide, width)
            recvs.append(pltpu.VMEM(shape, BF))
    depth = groups * 2 * np_
    dma = pltpu.SemaphoreType.DMA
    dims = (nsub, ni, np_, nb, nrow, ncol, nsep, nbits, plans)
    scratch = [
        pltpu.VMEM((2, ni, np_), BF),
        pltpu.VMEM((2, 2 * ni, nb), BF),
        pltpu.VMEM((2, 2 * ni, nb), BF),
        pltpu.VMEM((1024, np_), F32),
        pltpu.VMEM((groups, nrow - 1, 2, 2 * np_, nb), BF),
        pltpu.VMEM((groups, 2 * np_, wide), BF),
        pltpu.VMEM((groups, 2 * np_, wide), BF),
        pltpu.VMEM((wide, depth), BF),
        pltpu.VMEM((wide, depth), BF),
        pltpu.VMEM((depth, wide), BF),
        pltpu.VMEM((depth, wide), BF),
        pltpu.VMEM((2, nsep // 2, 2, wide, wide), BF),
        pltpu.VMEM((2, nrow - 1, nb, half), BF),
        *recvs,
        dma((2, 3)),
        dma((groups, nrow - 1, 2)),
        dma((groups, nrow - 1, 2)),
        dma((len(recvs),)),
        dma((len(recvs),)),
        dma((2, nrow - 1)),
        dma((2, nrow - 1)),
    ]
    hbm = pl.BlockSpec(memory_space=pl.ANY)
    vmem = pl.BlockSpec(memory_space=pltpu.VMEM)
    summed = pl.pallas_call(
        functools.partial(kernel, dims),
        out_shape=jax.ShapeDtypeStruct((2, nb, half), F32),
        in_specs=[pl.BlockSpec(memory_space=pltpu.SMEM), hbm, hbm, hbm, vmem, vmem],
        out_specs=vmem,
        scratch_shapes=scratch,
        compiler_params=pltpu.CompilerParams(
            collective_id=0, has_side_effects=True, vmem_limit_bytes=58 * 1024 * 1024
        ),
        name="modal_schur",
    )(sizes, phi, ck, cm, lam, sel)
    return k_bb + summed[0], m_bb + summed[1]


def solution(mesh):
    in_specs = (
        P("dom", None, "col"),
        P("dom", None, None, "row"),
        P("dom", None, None, "row"),
        P("dom", "col"),
        P("dom"),
        P("dom", None),
        P("dom", "row", "col"),
        P("dom", "row", "col"),
    )
    out_specs = (P("dom", "row", "col"), P("dom", "row", "col"))
    return jax.shard_map(
        per_device, mesh=mesh, in_specs=in_specs, out_specs=out_specs, check_vma=False
    )
```

```python
import functools

import jax
import jax.numpy as jnp
from jax import lax
from jax.experimental import pallas as pl
from jax.experimental.pallas import tpu as pltpu
from jax.sharding import PartitionSpec as P

MESH = pl.DeviceIdType.MESH
BF = jnp.bfloat16
F32 = jnp.float32


def kernel(dims, sizes_ref, phi_ref, ck_ref, cm_ref, lam_ref, sel_ref, out_ref,
           pbuf, kbuf, mbuf, rep, stage, coef_k, coef_m, sk_t, w_t, sk_r, w_r, part, acc, last, *rest):
    nsub, ni, np_, nb, nrow, ncol, nsep, nbits, plans = dims
    pieces = len(plans)
    steps = len(plans[0])
    nrecv = pieces * steps
    recvs = rest[:nrecv]
    (load_sem, send_sem, recv_sem, red_send, red_recv, last_send, last_recv) = rest[nrecv:]
    dom, row, col = lax.axis_index("dom"), lax.axis_index("row"), lax.axis_index("col")
    groups = nsub // nrow
    wide = nb * nrow
    half = wide // ncol
    cut = pieces // 2
    sub = nb // cut

    def partner(step):
        if step == "col":
            return (dom, row, 1 - col)
        bit = (dom // (1 << step)) % 2
        return (dom + (1 - 2 * bit) * (1 << step), row, col)

    def peer(k):
        return (dom, lax.rem(row + k, nrow), col)

    def loads(t, slot):
        s = (t // nrow) * nrow + lax.rem(row + 1 + lax.rem(t, nrow), nrow)
        return [
            pltpu.make_async_copy(phi_ref.at[s], pbuf.at[slot], load_sem.at[slot, 0]),
            pltpu.make_async_copy(ck_ref.at[s], kbuf.at[slot], load_sem.at[slot, 1]),
            pltpu.make_async_copy(cm_ref.at[s], mbuf.at[slot], load_sem.at[slot, 2]),
        ]

    for c in loads(0, 0):
        c.start()

    barrier = pltpu.get_barrier_semaphore()
    others = [peer(k) for k in range(1, nrow)] + [partner(b) for b in range(nbits)] + [partner("col")]
    for other in others:
        pl.semaphore_signal(barrier, inc=1, device_id=other, device_id_type=MESH)
    pl.semaphore_wait(barrier, len(others))

    chunk = 512
    lanes = lax.broadcasted_iota(jnp.int32, (1, 2 * chunk), 1) % 2
    even = (1 - lanes).astype(F32).astype(BF)
    odd = lanes.astype(F32).astype(BF)
    mine = pl.ds(pl.multiple_of(row * nb, 128), nb)

    def project(i, k, slot):
        t = i * nrow + k
        s = i * nrow + lax.rem(row + 1 + k, nrow)
        nxt = t + 1

        @pl.when(nxt < nsub)
        def _():
            for c in loads(nxt, 1 - slot):
                c.start()

        for c in loads(t, slot):
            c.wait()
        size = sizes_ref[s]

        def piece(h, acc):
            base = pl.multiple_of(h * chunk, chunk)
            rows = lax.broadcasted_iota(jnp.int32, (chunk, np_), 0) + base
            ph = pbuf[slot, pl.ds(base, chunk), :].astype(F32)
            ph = jnp.where(rows < size, ph, 0.0)
            rep[pl.ds(0, chunk, stride=2), :] = ph
            rep[pl.ds(1, chunk, stride=2), :] = ph
            rt = rep[...].astype(BF).T
            left = jnp.concatenate([rt * even, rt * odd], axis=0)
            base2 = pl.multiple_of(h * 2 * chunk, 2 * chunk)
            right = jnp.concatenate(
                [kbuf[slot, pl.ds(base2, 2 * chunk), :], mbuf[slot, pl.ds(base2, 2 * chunk), :]], axis=1
            )
            return acc + jnp.dot(left, right, preferred_element_type=F32)

        acc = lax.fori_loop(0, ni // chunk, piece, jnp.zeros((2 * np_, 2 * nb), F32))
        return acc.astype(BF)

    def sends(i, k):
        return [
            pltpu.make_async_remote_copy(
                src_ref=stage.at[i, k, q], dst_ref=dst.at[i, :, mine],
                send_sem=send_sem.at[i, k, q], recv_sem=recv_sem.at[i, k, q],
                device_id=peer(k + 1), device_id_type=MESH,
            )
            for q, dst in ((0, coef_k), (1, coef_m))
        ]

    def group(i, _):
        for k in range(nrow):
            val = project(i, k, k % 2)
            if k < nrow - 1:
                stage[i, k, 0] = val[:, :nb]
                stage[i, k, 1] = val[:, nb:]
                for c in sends(i, k):
                    c.start()
            else:
                coef_k[i, :, mine] = val[:, :nb]
                coef_m[i, :, mine] = val[:, nb:]
        return 0

    lax.fori_loop(0, groups, group, 0)

    for i in range(groups):
        for k in range(nrow - 1):
            for c in sends(i, k):
                c.wait()
        s = i * nrow + row
        for j in range(2):
            rows = slice(j * np_, (j + 1) * np_)
            at = (i * 2 + j) * np_
            inv = 1.0 / jnp.broadcast_to(lam_ref[pl.ds(s, 1), :], (128, np_)).T
            inv = jnp.concatenate([inv] * (wide // 128), axis=1)
            ck = coef_k[i, rows, :].astype(F32)
            cm = coef_m[i, rows, :].astype(F32)
            sk = ck * inv
            w = cm - 0.5 * sk
            sk_r[at:at + np_, :] = sk.astype(BF)
            w_r[at:at + np_, :] = w.astype(BF)
            sk_t[:, at:at + np_] = sk.T.astype(BF)
            w_t[:, at:at + np_] = w.T.astype(BF)

    depth = groups * 2 * np_

    def flat_k():
        return coef_k[...].reshape(depth, wide)

    def bit_of(step):
        return (dom // (1 << step)) % 2

    def gram(q, e, put):
        sel = sel_ref[row, pl.ds(e, 1), :].astype(BF)
        for a in range(0, wide, 256):
            lhs = sk_t[a:a + 256, :] * sel
            if q == 0:
                val = jnp.dot(lhs, flat_k(), preferred_element_type=F32)
            else:
                val = jnp.dot(lhs, w_r[...], preferred_element_type=F32)
                val += jnp.dot(w_t[a:a + 256, :] * sel, sk_r[...], preferred_element_type=F32)
            val = -val
            for b in range(0, 256, sub):
                r, h = (a + b) // nb, ((a + b) % nb) // sub
                put(q * cut + h, slice(r * sub, (r + 1) * sub), val[b:b + sub])

    def rcopy(p, n):
        step = plans[p][n]
        at = p * steps + n
        dst = recvs[at]
        if n == 0:
            send = part.at[p]
        elif step == "col":
            send = recvs[at - 1].at[:, :, :, pl.ds(pl.multiple_of((1 - col) * half, 128), half)]
        else:
            send = recvs[at - 1].at[:, 1 - bit_of(step)]
        if step != "col":
            a, b, r, c = dst.shape
            dst = dst.reshape(a * b, r, c)
        return pltpu.make_async_remote_copy(
            src_ref=send, dst_ref=dst, send_sem=red_send.at[at], recv_sem=red_recv.at[at],
            device_id=partner(step), device_id_type=MESH,
        )

    def combine(p, n):
        got = recvs[p * steps + n]
        a, b, _, width = got.shape
        done = [x for x in plans[p][1:n + 1] if x != "col"]
        base, stride = 0, 1
        for x in done:
            base, stride = base + stride * bit_of(x), stride * 2
        first = 0 if width == wide else pl.multiple_of(col * half, 128)
        full = pl.ds(first, width)
        step = plans[p][n + 1] if n + 1 < steps else None
        for x in range(a):
            if step is None:
                tot = acc[p, base, :, full] + got[0, 0].astype(F32)
                acc[p, base, :, full] = tot
                got[0, 0] = tot.astype(BF)
            elif step == "col":
                for y in range(b):
                    at = base + (x * b + y) * stride
                    own = pl.ds(pl.multiple_of(col * half, 128), half)
                    away = pl.ds(pl.multiple_of((1 - col) * half, 128), half)
                    got[x, y, :, away] = (acc[p, at, :, away] + got[x, y, :, away].astype(F32)).astype(BF)
                    acc[p, at, :, own] += got[x, y, :, own].astype(F32)
            else:
                keep = bit_of(step)
                away = 1 - keep
                at = base + (2 * x + away) * stride
                got[x, away] = (acc[p, at, :, full] + got[x, away].astype(F32)).astype(BF)
                at = base + (2 * x + keep) * stride
                acc[p, at, :, full] += got[x, keep].astype(F32)

    def lcopy(p, k):
        to = lax.rem(row + k, nrow)
        return pltpu.make_async_remote_copy(
            src_ref=recvs[p * steps + steps - 1].at[0, 0, pl.ds(pl.multiple_of(to * sub, sub), sub), :],
            dst_ref=last.at[p, k - 1],
            send_sem=last_send.at[p, k - 1], recv_sem=last_recv.at[p, k - 1],
            device_id=peer(k), device_id_type=MESH,
        )

    low = dom % 2
    for q in range(2):
        @pl.loop(0, nsep // 2)
        def _(x):
            def put(p, rows, val):
                part[p, x, rows, :] = val.astype(BF)

            gram(q, 2 * x + 1 - low, put)

        for h in range(cut):
            rcopy(q * cut + h, 0).start()
    for q in range(2):
        @pl.loop(0, nsep // 2)
        def _(x):
            def put(p, rows, val):
                acc[p, x, rows, :] = val

            gram(q, 2 * x + low, put)

    order = [q * cut + h for h in range(cut) for q in range(2)]
    for n in range(steps):
        for p in order:
            rcopy(p, n).wait_recv()
            combine(p, n)
            if n + 1 < steps:
                rcopy(p, n + 1).start()
            else:
                for k in range(1, nrow):
                    lcopy(p, k).start()
    kept = dom // 2
    tile = pl.ds(pl.multiple_of(row * sub, sub), sub)
    for p in order:
        total = acc[p, kept, tile, pl.ds(pl.multiple_of(col * half, 128), half)]
        for k in range(1, nrow):
            lcopy(p, k).wait()
            total += last[p, k - 1].astype(F32)
        h = p % cut
        out_ref[p // cut, h * sub:(h + 1) * sub, :] = total
        for n in range(steps):
            rcopy(p, n).wait_send()


def per_device(phi, couple_k, couple_m, eigen, sizes, adjacency, k_bb, m_bb):
    nsub, ni, np_ = phi.shape
    nb = couple_k.shape[3]
    nrow, ncol, nsep = lax.axis_size("row"), lax.axis_size("col"), lax.axis_size("dom")
    nbits = nsep.bit_length() - 1
    wide = nb * nrow
    half = wide // ncol
    groups = nsub // nrow
    ck = couple_k.reshape(nsub, 2 * ni, nb)
    cm = couple_m.reshape(nsub, 2 * ni, nb)
    sel = (adjacency[None] == lax.broadcasted_iota(jnp.int32, (nsep, 1, 1), 0)).astype(F32)
    sel = sel.reshape(nsep, groups, nrow, 2).transpose(2, 0, 1, 3)
    sel = jnp.repeat(sel.reshape(nrow, nsep, groups * 2), np_, axis=2)
    cut = 2
    rows = wide // cut
    plans = (tuple(range(nbits)) + ("col",),) * cut + ((0, "col") + tuple(range(1, nbits)),) * cut
    recvs = []
    for plan in plans:
        count, width = nsep, wide
        for n, step in enumerate(plan):
            if step == "col":
                width = half
            else:
                count //= 2
            later = [x for x in plan[n + 1:] if x != "col"]
            shape = (count // 2, 2, rows, width) if later else (1, 1, rows, width)
            recvs.append(pltpu.VMEM(shape, BF))
    depth = groups * 2 * np_
    dma = pltpu.SemaphoreType.DMA
    dims = (nsub, ni, np_, nb, nrow, ncol, nsep, nbits, plans)
    scratch = [
        pltpu.VMEM((2, ni, np_), BF),
        pltpu.VMEM((2, 2 * ni, nb), BF),
        pltpu.VMEM((2, 2 * ni, nb), BF),
        pltpu.VMEM((1024, np_), F32),
        pltpu.VMEM((groups, nrow - 1, 2, 2 * np_, nb), BF),
        pltpu.VMEM((groups, 2 * np_, wide), BF),
        pltpu.VMEM((groups, 2 * np_, wide), BF),
        pltpu.VMEM((wide, depth), BF),
        pltpu.VMEM((wide, depth), BF),
        pltpu.VMEM((depth, wide), BF),
        pltpu.VMEM((depth, wide), BF),
        pltpu.VMEM((2 * cut, nsep // 2, rows, wide), BF),
        pltpu.VMEM((2 * cut, nsep // 2, rows, wide), F32),
        pltpu.VMEM((2 * cut, nrow - 1, nb // cut, half), BF),
        *recvs,
        dma((2, 3)),
        dma((groups, nrow - 1, 2)),
        dma((groups, nrow - 1, 2)),
        dma((len(recvs),)),
        dma((len(recvs),)),
        dma((2 * cut, nrow - 1)),
        dma((2 * cut, nrow - 1)),
    ]
    hbm = pl.BlockSpec(memory_space=pl.ANY)
    vmem = pl.BlockSpec(memory_space=pltpu.VMEM)
    summed = pl.pallas_call(
        functools.partial(kernel, dims),
        out_shape=jax.ShapeDtypeStruct((2, nb, half), F32),
        in_specs=[pl.BlockSpec(memory_space=pltpu.SMEM), hbm, hbm, hbm, vmem, vmem],
        out_specs=vmem,
        scratch_shapes=scratch,
        compiler_params=pltpu.CompilerParams(
            collective_id=0, has_side_effects=True, vmem_limit_bytes=58 * 1024 * 1024
        ),
        name="modal_schur",
    )(sizes, phi, ck, cm, eigen, sel)
    return k_bb + summed[0], m_bb + summed[1]


def solution(mesh):
    in_specs = (
        P("dom", None, "col"),
        P("dom", None, None, "row"),
        P("dom", None, None, "row"),
        P("dom", "col"),
        P("dom"),
        P("dom", None),
        P("dom", "row", "col"),
        P("dom", "row", "col"),
    )
    out_specs = (P("dom", "row", "col"), P("dom", "row", "col"))
    return jax.shard_map(
        per_device, mesh=mesh, in_specs=in_specs, out_specs=out_specs, check_vma=False
    )
```

```python
import functools

import jax
import jax.numpy as jnp
from jax import lax
from jax.experimental import pallas as pl
from jax.experimental.pallas import tpu as pltpu
from jax.sharding import PartitionSpec as P

MESH = pl.DeviceIdType.MESH
BF = jnp.bfloat16
F32 = jnp.float32


def kernel(dims, sizes_ref, phi_ref, ck_ref, cm_ref, lam_ref, sel_ref, out_ref,
           pbuf, kbuf, mbuf, rep, stage, coef_k, coef_m, sk_t, w_t, sk_r, w_r, part, acc, early, last, *rest):
    nsub, ni, np_, nb, nrow, ncol, nsep, nbits, plans = dims
    pieces = len(plans)
    steps = len(plans[0])
    nrecv = pieces * steps
    recvs = rest[:nrecv]
    (load_sem, send_sem, recv_sem, red_send, red_recv, last_send, last_recv) = rest[nrecv:]
    dom, row, col = lax.axis_index("dom"), lax.axis_index("row"), lax.axis_index("col")
    groups = nsub // nrow
    wide = nb * nrow
    half = wide // ncol
    cut = pieces // 2
    sub = nb // cut

    def partner(step):
        if step == "col":
            return (dom, row, 1 - col)
        bit = (dom // (1 << step)) % 2
        return (dom + (1 - 2 * bit) * (1 << step), row, col)

    def peer(k):
        return (dom, lax.rem(row + k, nrow), col)

    def loads(t, slot):
        s = (t // nrow) * nrow + lax.rem(row + 1 + lax.rem(t, nrow), nrow)
        return [
            pltpu.make_async_copy(phi_ref.at[s], pbuf.at[slot], load_sem.at[slot, 0]),
            pltpu.make_async_copy(ck_ref.at[s], kbuf.at[slot], load_sem.at[slot, 1]),
            pltpu.make_async_copy(cm_ref.at[s], mbuf.at[slot], load_sem.at[slot, 2]),
        ]

    for c in loads(0, 0):
        c.start()

    barrier = pltpu.get_barrier_semaphore()
    others = [peer(k) for k in range(1, nrow)] + [partner(b) for b in range(nbits)] + [partner("col")]
    for other in others:
        pl.semaphore_signal(barrier, inc=1, device_id=other, device_id_type=MESH)
    pl.semaphore_wait(barrier, len(others))

    chunk = 1024
    lanes = lax.broadcasted_iota(jnp.int32, (1, 2 * chunk), 1) % 2
    even = (1 - lanes).astype(F32).astype(BF)
    odd = lanes.astype(F32).astype(BF)
    mine = pl.ds(pl.multiple_of(row * nb, 128), nb)

    def project(i, k, slot):
        t = i * nrow + k
        s = i * nrow + lax.rem(row + 1 + k, nrow)
        nxt = t + 1

        @pl.when(nxt < nsub)
        def _():
            for c in loads(nxt, 1 - slot):
                c.start()

        for c in loads(t, slot):
            c.wait()
        size = sizes_ref[s]

        def piece(h, acc):
            base = pl.multiple_of(h * chunk, chunk)
            rows = lax.broadcasted_iota(jnp.int32, (chunk, np_), 0) + base
            ph = pbuf[slot, pl.ds(base, chunk), :].astype(F32)
            ph = jnp.where(rows < size, ph, 0.0)
            rep[pl.ds(0, chunk, stride=2), :] = ph
            rep[pl.ds(1, chunk, stride=2), :] = ph
            rt = rep[...].astype(BF).T
            left = jnp.concatenate([rt * even, rt * odd], axis=0)
            base2 = pl.multiple_of(h * 2 * chunk, 2 * chunk)
            right = jnp.concatenate(
                [kbuf[slot, pl.ds(base2, 2 * chunk), :], mbuf[slot, pl.ds(base2, 2 * chunk), :]], axis=1
            )
            return acc + jnp.dot(left, right, preferred_element_type=F32)

        acc = lax.fori_loop(0, ni // chunk, piece, jnp.zeros((2 * np_, 2 * nb), F32))
        return acc.astype(BF)

    def sends(i, k):
        return [
            pltpu.make_async_remote_copy(
                src_ref=stage.at[i, k, q], dst_ref=dst.at[i, :, mine],
                send_sem=send_sem.at[i, k, q], recv_sem=recv_sem.at[i, k, q],
                device_id=peer(k + 1), device_id_type=MESH,
            )
            for q, dst in ((0, coef_k), (1, coef_m))
        ]

    def group(i, _):
        for k in range(nrow):
            val = project(i, k, k % 2)
            if k < nrow - 1:
                stage[i, k, 0] = val[:, :nb]
                stage[i, k, 1] = val[:, nb:]
                for c in sends(i, k):
                    c.start()
            else:
                coef_k[i, :, mine] = val[:, :nb]
                coef_m[i, :, mine] = val[:, nb:]
        return 0

    lax.fori_loop(0, groups, group, 0)

    span = 2 * np_
    depth = groups * span
    head = depth - span
    hold = early.shape[1] == nsep // 2

    def prepare(i):
        for k in range(nrow - 1):
            for c in sends(i, k):
                c.wait()
        s = i * nrow + row
        inv = 1.0 / jnp.broadcast_to(lam_ref[pl.ds(s, 1), :], (128, np_)).T
        inv = jnp.concatenate([inv] * (wide // 128), axis=1)
        for j in range(2):
            rows = slice(j * np_, (j + 1) * np_)
            at = i * span + j * np_
            ck = coef_k[i, rows, :].astype(F32)
            cm = coef_m[i, rows, :].astype(F32)
            sk = ck * inv
            w = cm - 0.5 * sk
            sk_r[at:at + np_, :] = sk.astype(BF)
            w_r[at:at + np_, :] = w.astype(BF)
            sk_t[:, at:at + np_] = sk.T.astype(BF)
            w_t[:, at:at + np_] = w.T.astype(BF)

    def bit_of(step):
        return (dom // (1 << step)) % 2

    def gram(q, e, lo, hi, put):
        sel = sel_ref[row, pl.ds(e, 1), :].astype(BF)[:, lo:hi]
        for a in range(0, wide, 256):
            lhs = sk_t[a:a + 256, lo:hi] * sel
            if q == 0:
                val = jnp.dot(
                    lhs, coef_k[lo // span:hi // span].reshape(hi - lo, wide), preferred_element_type=F32
                )
            else:
                val = jnp.dot(lhs, w_r[lo:hi, :], preferred_element_type=F32)
                val += jnp.dot(w_t[a:a + 256, lo:hi] * sel, sk_r[lo:hi, :], preferred_element_type=F32)
            val = -val
            for b in range(0, 256, sub):
                r, h = (a + b) // nb, ((a + b) % nb) // sub
                put(q * cut + h, slice(r * sub, (r + 1) * sub), val[b:b + sub])

    def rcopy(p, n):
        step = plans[p][n]
        at = p * steps + n
        dst = recvs[at]
        if n == 0:
            send = part.at[p]
        elif step == "col":
            send = recvs[at - 1].at[:, :, :, pl.ds(pl.multiple_of((1 - col) * half, 128), half)]
        else:
            send = recvs[at - 1].at[:, 1 - bit_of(step)]
        if step != "col":
            a, b, r, c = dst.shape
            dst = dst.reshape(a * b, r, c)
        return pltpu.make_async_remote_copy(
            src_ref=send, dst_ref=dst, send_sem=red_send.at[at], recv_sem=red_recv.at[at],
            device_id=partner(step), device_id_type=MESH,
        )

    def combine(p, n):
        got = recvs[p * steps + n]
        a, b, _, width = got.shape
        done = [x for x in plans[p][1:n + 1] if x != "col"]
        base, stride = 0, 1
        for x in done:
            base, stride = base + stride * bit_of(x), stride * 2
        first = 0 if width == wide else pl.multiple_of(col * half, 128)
        full = pl.ds(first, width)
        step = plans[p][n + 1] if n + 1 < steps else None
        for x in range(a):
            if step is None:
                tot = acc[p, base, :, full] + got[0, 0].astype(F32)
                acc[p, base, :, full] = tot
                got[0, 0] = tot.astype(BF)
            elif step == "col":
                for y in range(b):
                    at = base + (x * b + y) * stride
                    own = pl.ds(pl.multiple_of(col * half, 128), half)
                    away = pl.ds(pl.multiple_of((1 - col) * half, 128), half)
                    got[x, y, :, away] = (acc[p, at, :, away] + got[x, y, :, away].astype(F32)).astype(BF)
                    acc[p, at, :, own] += got[x, y, :, own].astype(F32)
            else:
                keep = bit_of(step)
                away = 1 - keep
                at = base + (2 * x + away) * stride
                got[x, away] = (acc[p, at, :, full] + got[x, away].astype(F32)).astype(BF)
                at = base + (2 * x + keep) * stride
                acc[p, at, :, full] += got[x, keep].astype(F32)

    def lcopy(p, k):
        to = lax.rem(row + k, nrow)
        return pltpu.make_async_remote_copy(
            src_ref=recvs[p * steps + steps - 1].at[0, 0, pl.ds(pl.multiple_of(to * sub, sub), sub), :],
            dst_ref=last.at[p, k - 1],
            send_sem=last_send.at[p, k - 1], recv_sem=last_recv.at[p, k - 1],
            device_id=peer(k), device_id_type=MESH,
        )

    low = dom % 2
    for i in range(groups - 1):
        prepare(i)
    for q in range(2):
        @pl.loop(0, nsep // 2)
        def _(x):
            def put(p, rows, val):
                acc[p, x, rows, :] = val

            def put_early(p, rows, val):
                early[p, x, rows, :] = val

            if head > 0:
                gram(q, 2 * x + low, 0, head, put)
                if hold:
                    gram(q, 2 * x + 1 - low, 0, head, put_early)

    prepare(groups - 1)
    begun = hold and head > 0
    for q in range(2):
        @pl.loop(0, nsep // 2)
        def _(x):
            def put(p, rows, val):
                if begun:
                    val = val + early[p, x, rows, :]
                part[p, x, rows, :] = val.astype(BF)

            gram(q, 2 * x + 1 - low, head if begun else 0, depth, put)

        for h in range(cut):
            rcopy(q * cut + h, 0).start()
    for q in range(2):
        @pl.loop(0, nsep // 2)
        def _(x):
            def put(p, rows, val):
                if head > 0:
                    val = val + acc[p, x, rows, :]
                acc[p, x, rows, :] = val

            gram(q, 2 * x + low, head, depth, put)

    order = [q * cut + h for h in range(cut) for q in range(2)]
    for n in range(steps):
        for p in order:
            rcopy(p, n).wait_recv()
            combine(p, n)
            if n + 1 < steps:
                rcopy(p, n + 1).start()
            else:
                for k in range(1, nrow):
                    lcopy(p, k).start()
    kept = dom // 2
    tile = pl.ds(pl.multiple_of(row * sub, sub), sub)
    for p in order:
        total = acc[p, kept, tile, pl.ds(pl.multiple_of(col * half, 128), half)]
        for k in range(1, nrow):
            lcopy(p, k).wait()
            total += last[p, k - 1].astype(F32)
        h = p % cut
        out_ref[p // cut, h * sub:(h + 1) * sub, :] = total
        for n in range(steps):
            rcopy(p, n).wait_send()


def per_device(phi, couple_k, couple_m, eigen, sizes, adjacency, k_bb, m_bb):
    nsub, ni, np_ = phi.shape
    nb = couple_k.shape[3]
    nrow, ncol, nsep = lax.axis_size("row"), lax.axis_size("col"), lax.axis_size("dom")
    nbits = nsep.bit_length() - 1
    wide = nb * nrow
    half = wide // ncol
    groups = nsub // nrow
    ck = couple_k.reshape(nsub, 2 * ni, nb)
    cm = couple_m.reshape(nsub, 2 * ni, nb)
    sel = (adjacency[None] == lax.broadcasted_iota(jnp.int32, (nsep, 1, 1), 0)).astype(F32)
    sel = sel.reshape(nsep, groups, nrow, 2).transpose(2, 0, 1, 3)
    sel = jnp.repeat(sel.reshape(nrow, nsep, groups * 2), np_, axis=2)
    cut = 2
    rows = wide // cut
    plans = (tuple(range(nbits)) + ("col",),) * cut + ((0, "col") + tuple(range(1, nbits)),) * cut
    recvs = []
    for plan in plans:
        count, width = nsep, wide
        for n, step in enumerate(plan):
            if step == "col":
                width = half
            else:
                count //= 2
            later = [x for x in plan[n + 1:] if x != "col"]
            shape = (count // 2, 2, rows, width) if later else (1, 1, rows, width)
            recvs.append(pltpu.VMEM(shape, BF))
    depth = groups * 2 * np_
    dma = pltpu.SemaphoreType.DMA
    dims = (nsub, ni, np_, nb, nrow, ncol, nsep, nbits, plans)
    scratch = [
        pltpu.VMEM((2, ni, np_), BF),
        pltpu.VMEM((2, 2 * ni, nb), BF),
        pltpu.VMEM((2, 2 * ni, nb), BF),
        pltpu.VMEM((2048, np_), F32),
        pltpu.VMEM((groups, nrow - 1, 2, 2 * np_, nb), BF),
        pltpu.VMEM((groups, 2 * np_, wide), BF),
        pltpu.VMEM((groups, 2 * np_, wide), BF),
        pltpu.VMEM((wide, depth), BF),
        pltpu.VMEM((wide, depth), BF),
        pltpu.VMEM((depth, wide), BF),
        pltpu.VMEM((depth, wide), BF),
        pltpu.VMEM((2 * cut, nsep // 2, rows, wide), BF),
        pltpu.VMEM((2 * cut, nsep // 2, rows, wide), F32),
        pltpu.VMEM((2 * cut, nsep // 2, rows, wide) if nsep <= 4 else (1, 1, 8, 128), F32),
        pltpu.VMEM((2 * cut, nrow - 1, nb // cut, half), BF),
        *recvs,
        dma((2, 3)),
        dma((groups, nrow - 1, 2)),
        dma((groups, nrow - 1, 2)),
        dma((len(recvs),)),
        dma((len(recvs),)),
        dma((2 * cut, nrow - 1)),
        dma((2 * cut, nrow - 1)),
    ]
    hbm = pl.BlockSpec(memory_space=pl.ANY)
    vmem = pl.BlockSpec(memory_space=pltpu.VMEM)
    summed = pl.pallas_call(
        functools.partial(kernel, dims),
        out_shape=jax.ShapeDtypeStruct((2, nb, half), F32),
        in_specs=[pl.BlockSpec(memory_space=pltpu.SMEM), hbm, hbm, hbm, vmem, vmem],
        out_specs=vmem,
        scratch_shapes=scratch,
        compiler_params=pltpu.CompilerParams(
            collective_id=0, has_side_effects=True, vmem_limit_bytes=58 * 1024 * 1024
        ),
        name="modal_schur",
    )(sizes, phi, ck, cm, eigen, sel)
    return k_bb + summed[0], m_bb + summed[1]


def solution(mesh):
    in_specs = (
        P("dom", None, "col"),
        P("dom", None, None, "row"),
        P("dom", None, None, "row"),
        P("dom", "col"),
        P("dom"),
        P("dom", None),
        P("dom", "row", "col"),
        P("dom", "row", "col"),
    )
    out_specs = (P("dom", "row", "col"), P("dom", "row", "col"))
    return jax.shard_map(
        per_device, mesh=mesh, in_specs=in_specs, out_specs=out_specs, check_vma=False
    )
```

```python
import functools

import jax
import jax.numpy as jnp
from jax import lax
from jax.experimental import pallas as pl
from jax.experimental.pallas import tpu as pltpu
from jax.sharding import PartitionSpec as P

MESH = pl.DeviceIdType.MESH
BF = jnp.bfloat16
F32 = jnp.float32


def kernel(dims, sizes_ref, phi_ref, ck_ref, cm_ref, lam_ref, sel_ref, out_ref,
           pbuf, kbuf, mbuf, rep, stage, coef_k, coef_m, sk_t, w_t, sk_r, w_r, part, acc, early, last, *rest):
    nsub, ni, np_, nb, nrow, ncol, nsep, nbits, plans = dims
    pieces = len(plans)
    steps = len(plans[0])
    nrecv = pieces * steps
    recvs = rest[:nrecv]
    (load_sem, send_sem, recv_sem, red_send, red_recv, last_send, last_recv) = rest[nrecv:]
    dom, row, col = lax.axis_index("dom"), lax.axis_index("row"), lax.axis_index("col")
    groups = nsub // nrow
    wide = nb * nrow
    half = wide // ncol
    cut = pieces // 2
    sub = nb // cut

    def partner(step):
        if step == "col":
            return (dom, row, 1 - col)
        bit = (dom // (1 << step)) % 2
        return (dom + (1 - 2 * bit) * (1 << step), row, col)

    def peer(k):
        return (dom, lax.rem(row + k, nrow), col)

    def loads(t, slot):
        s = (t // nrow) * nrow + lax.rem(row + 1 + lax.rem(t, nrow), nrow)
        return [
            pltpu.make_async_copy(phi_ref.at[s], pbuf.at[slot], load_sem.at[slot, 0]),
            pltpu.make_async_copy(ck_ref.at[s], kbuf.at[slot], load_sem.at[slot, 1]),
            pltpu.make_async_copy(cm_ref.at[s], mbuf.at[slot], load_sem.at[slot, 2]),
        ]

    for c in loads(0, 0):
        c.start()

    barrier = pltpu.get_barrier_semaphore()
    others = [peer(k) for k in range(1, nrow)] + [partner(b) for b in range(nbits)] + [partner("col")]
    for other in others:
        pl.semaphore_signal(barrier, inc=1, device_id=other, device_id_type=MESH)
    pl.semaphore_wait(barrier, len(others))

    chunk = 1024
    lanes = lax.broadcasted_iota(jnp.int32, (1, 2 * chunk), 1) % 2
    even = (1 - lanes).astype(F32).astype(BF)
    odd = lanes.astype(F32).astype(BF)
    mine = pl.ds(pl.multiple_of(row * nb, 128), nb)

    def project(i, k, slot):
        t = i * nrow + k
        s = i * nrow + lax.rem(row + 1 + k, nrow)
        nxt = t + 1

        @pl.when(nxt < nsub)
        def _():
            for c in loads(nxt, 1 - slot):
                c.start()

        for c in loads(t, slot):
            c.wait()
        size = sizes_ref[s]

        def piece(h, acc):
            base = pl.multiple_of(h * chunk, chunk)
            rows = lax.broadcasted_iota(jnp.int32, (chunk, np_), 0) + base
            ph = pbuf[slot, pl.ds(base, chunk), :].astype(F32)
            ph = jnp.where(rows < size, ph, 0.0)
            rep[pl.ds(0, chunk, stride=2), :] = ph
            rep[pl.ds(1, chunk, stride=2), :] = ph
            rt = rep[...].astype(BF).T
            left = jnp.concatenate([rt * even, rt * odd], axis=0)
            base2 = pl.multiple_of(h * 2 * chunk, 2 * chunk)
            right = jnp.concatenate(
                [kbuf[slot, pl.ds(base2, 2 * chunk), :], mbuf[slot, pl.ds(base2, 2 * chunk), :]], axis=1
            )
            return acc + jnp.dot(left, right, preferred_element_type=F32)

        acc = lax.fori_loop(0, ni // chunk, piece, jnp.zeros((2 * np_, 2 * nb), F32))
        return acc.astype(BF)

    def sends(i, k):
        return [
            pltpu.make_async_remote_copy(
                src_ref=stage.at[i, k, q], dst_ref=dst.at[i, :, mine],
                send_sem=send_sem.at[i, k, q], recv_sem=recv_sem.at[i, k, q],
                device_id=peer(k + 1), device_id_type=MESH,
            )
            for q, dst in ((0, coef_k), (1, coef_m))
        ]

    def group(i, _):
        for k in range(nrow):
            val = project(i, k, k % 2)
            if k < nrow - 1:
                stage[i, k, 0] = val[:, :nb]
                stage[i, k, 1] = val[:, nb:]
                for c in sends(i, k):
                    c.start()
            else:
                coef_k[i, :, mine] = val[:, :nb]
                coef_m[i, :, mine] = val[:, nb:]
        return 0

    lax.fori_loop(0, groups, group, 0)

    span = 2 * np_
    depth = groups * span
    head = depth - span
    hold = early.shape[1] == nsep // 2

    def prepare(i):
        for k in range(nrow - 1):
            for c in sends(i, k):
                c.wait()
        s = i * nrow + row
        inv = 1.0 / jnp.broadcast_to(lam_ref[pl.ds(s, 1), :], (128, np_)).T
        inv = jnp.concatenate([inv] * (wide // 128), axis=1)
        for j in range(2):
            rows = slice(j * np_, (j + 1) * np_)
            at = i * span + j * np_
            ck = coef_k[i, rows, :].astype(F32)
            cm = coef_m[i, rows, :].astype(F32)
            sk = ck * inv
            w = cm - 0.5 * sk
            sk_r[at:at + np_, :] = sk.astype(BF)
            w_r[at:at + np_, :] = w.astype(BF)
            sk_t[:, at:at + np_] = sk.T.astype(BF)
            w_t[:, at:at + np_] = w.T.astype(BF)

    def bit_of(step):
        return (dom // (1 << step)) % 2

    def gram(q, e, lo, hi, put):
        sel = sel_ref[row, pl.ds(e, 1), :].astype(BF)[:, lo:hi]
        for a in range(0, wide, 256):
            lhs = sk_t[a:a + 256, lo:hi] * sel
            if q == 0:
                val = jnp.dot(
                    lhs, coef_k[lo // span:hi // span].reshape(hi - lo, wide), preferred_element_type=F32
                )
            else:
                val = jnp.dot(lhs, w_r[lo:hi, :], preferred_element_type=F32)
                val += jnp.dot(w_t[a:a + 256, lo:hi] * sel, sk_r[lo:hi, :], preferred_element_type=F32)
            val = -val
            for b in range(0, 256, sub):
                r, h = (a + b) // nb, ((a + b) % nb) // sub
                put(q * cut + h, slice(r * sub, (r + 1) * sub), val[b:b + sub])

    def rcopy(p, n):
        step = plans[p][n]
        at = p * steps + n
        dst = recvs[at]
        if n == 0:
            send = part.at[p]
        elif step == "col":
            send = recvs[at - 1].at[:, :, :, pl.ds(pl.multiple_of((1 - col) * half, 128), half)]
        else:
            send = recvs[at - 1].at[:, 1 - bit_of(step)]
        if step != "col":
            a, b, r, c = dst.shape
            dst = dst.reshape(a * b, r, c)
        return pltpu.make_async_remote_copy(
            src_ref=send, dst_ref=dst, send_sem=red_send.at[at], recv_sem=red_recv.at[at],
            device_id=partner(step), device_id_type=MESH,
        )

    def combine(p, n):
        got = recvs[p * steps + n]
        a, b, _, width = got.shape
        done = [x for x in plans[p][1:n + 1] if x != "col"]
        base, stride = 0, 1
        for x in done:
            base, stride = base + stride * bit_of(x), stride * 2
        first = 0 if width == wide else pl.multiple_of(col * half, 128)
        full = pl.ds(first, width)
        step = plans[p][n + 1] if n + 1 < steps else None
        for x in range(a):
            if step is None:
                tot = acc[p, base, :, full] + got[0, 0].astype(F32)
                acc[p, base, :, full] = tot
                got[0, 0] = tot.astype(BF)
            elif step == "col":
                for y in range(b):
                    at = base + (x * b + y) * stride
                    own = pl.ds(pl.multiple_of(col * half, 128), half)
                    away = pl.ds(pl.multiple_of((1 - col) * half, 128), half)
                    got[x, y, :, away] = (acc[p, at, :, away] + got[x, y, :, away].astype(F32)).astype(BF)
                    acc[p, at, :, own] += got[x, y, :, own].astype(F32)
            else:
                keep = bit_of(step)
                away = 1 - keep
                at = base + (2 * x + away) * stride
                got[x, away] = (acc[p, at, :, full] + got[x, away].astype(F32)).astype(BF)
                at = base + (2 * x + keep) * stride
                acc[p, at, :, full] += got[x, keep].astype(F32)

    def lcopy(p, k):
        to = lax.rem(row + k, nrow)
        return pltpu.make_async_remote_copy(
            src_ref=recvs[p * steps + steps - 1].at[0, 0, pl.ds(pl.multiple_of(to * sub, sub), sub), :],
            dst_ref=last.at[p, k - 1],
            send_sem=last_send.at[p, k - 1], recv_sem=last_recv.at[p, k - 1],
            device_id=peer(k), device_id_type=MESH,
        )

    low = dom % 2
    for i in range(groups - 1):
        prepare(i)
    for q in range(2):
        @pl.loop(0, nsep // 2)
        def _(x):
            def put(p, rows, val):
                acc[p, x, rows, :] = val

            def put_early(p, rows, val):
                early[p, x, rows, :] = val

            if head > 0:
                gram(q, 2 * x + low, 0, head, put)
                if hold:
                    gram(q, 2 * x + 1 - low, 0, head, put_early)

    prepare(groups - 1)
    begun = hold and head > 0
    for q in range(2):
        @pl.loop(0, nsep // 2)
        def _(x):
            def put(p, rows, val):
                if begun:
                    val = val + early[p, x, rows, :]
                part[p, x, rows, :] = val.astype(BF)

            gram(q, 2 * x + 1 - low, head if begun else 0, depth, put)

        for h in range(cut):
            rcopy(q * cut + h, 0).start()
    for q in range(2):
        @pl.loop(0, nsep // 2)
        def _(x):
            def put(p, rows, val):
                if head > 0:
                    val = val + acc[p, x, rows, :]
                acc[p, x, rows, :] = val

            gram(q, 2 * x + low, head, depth, put)

    order = [q * cut + h for h in range(cut) for q in range(2)]
    for n in range(steps):
        for p in order:
            rcopy(p, n).wait_recv()
            combine(p, n)
            if n + 1 < steps:
                rcopy(p, n + 1).start()
            else:
                for k in range(1, nrow):
                    lcopy(p, k).start()
    kept = dom // 2
    tile = pl.ds(pl.multiple_of(row * sub, sub), sub)
    for p in order:
        total = acc[p, kept, tile, pl.ds(pl.multiple_of(col * half, 128), half)]
        for k in range(1, nrow):
            lcopy(p, k).wait()
            total += last[p, k - 1].astype(F32)
        h = p % cut
        out_ref[p // cut, h * sub:(h + 1) * sub, :] = total
        for n in range(steps):
            rcopy(p, n).wait_send()


def per_device(phi, couple_k, couple_m, eigen, sizes, adjacency, k_bb, m_bb):
    nsub, ni, np_ = phi.shape
    nb = couple_k.shape[3]
    nrow, ncol, nsep = lax.axis_size("row"), lax.axis_size("col"), lax.axis_size("dom")
    nbits = nsep.bit_length() - 1
    wide = nb * nrow
    half = wide // ncol
    groups = nsub // nrow
    ck = couple_k.reshape(nsub, 2 * ni, nb)
    cm = couple_m.reshape(nsub, 2 * ni, nb)
    sel = (adjacency[None] == lax.broadcasted_iota(jnp.int32, (nsep, 1, 1), 0)).astype(F32)
    sel = sel.reshape(nsep, groups, nrow, 2).transpose(2, 0, 1, 3)
    sel = jnp.repeat(sel.reshape(nrow, nsep, groups * 2), np_, axis=2)
    cut = 4
    rows = wide // cut
    plans = (tuple(range(nbits)) + ("col",),) * cut + ((0, "col") + tuple(range(1, nbits)),) * cut
    recvs = []
    for plan in plans:
        count, width = nsep, wide
        for n, step in enumerate(plan):
            if step == "col":
                width = half
            else:
                count //= 2
            later = [x for x in plan[n + 1:] if x != "col"]
            shape = (count // 2, 2, rows, width) if later else (1, 1, rows, width)
            recvs.append(pltpu.VMEM(shape, BF))
    depth = groups * 2 * np_
    dma = pltpu.SemaphoreType.DMA
    dims = (nsub, ni, np_, nb, nrow, ncol, nsep, nbits, plans)
    scratch = [
        pltpu.VMEM((2, ni, np_), BF),
        pltpu.VMEM((2, 2 * ni, nb), BF),
        pltpu.VMEM((2, 2 * ni, nb), BF),
        pltpu.VMEM((2048, np_), F32),
        pltpu.VMEM((groups, nrow - 1, 2, 2 * np_, nb), BF),
        pltpu.VMEM((groups, 2 * np_, wide), BF),
        pltpu.VMEM((groups, 2 * np_, wide), BF),
        pltpu.VMEM((wide, depth), BF),
        pltpu.VMEM((wide, depth), BF),
        pltpu.VMEM((depth, wide), BF),
        pltpu.VMEM((depth, wide), BF),
        pltpu.VMEM((2 * cut, nsep // 2, rows, wide), BF),
        pltpu.VMEM((2 * cut, nsep // 2, rows, wide), F32),
        pltpu.VMEM((2 * cut, nsep // 2, rows, wide) if nsep <= 4 else (1, 1, 8, 128), F32),
        pltpu.VMEM((2 * cut, nrow - 1, nb // cut, half), BF),
        *recvs,
        dma((2, 3)),
        dma((groups, nrow - 1, 2)),
        dma((groups, nrow - 1, 2)),
        dma((len(recvs),)),
        dma((len(recvs),)),
        dma((2 * cut, nrow - 1)),
        dma((2 * cut, nrow - 1)),
    ]
    hbm = pl.BlockSpec(memory_space=pl.ANY)
    vmem = pl.BlockSpec(memory_space=pltpu.VMEM)
    summed = pl.pallas_call(
        functools.partial(kernel, dims),
        out_shape=jax.ShapeDtypeStruct((2, nb, half), F32),
        in_specs=[pl.BlockSpec(memory_space=pltpu.SMEM), hbm, hbm, hbm, vmem, vmem],
        out_specs=vmem,
        scratch_shapes=scratch,
        compiler_params=pltpu.CompilerParams(
            collective_id=0, has_side_effects=True, vmem_limit_bytes=58 * 1024 * 1024
        ),
        name="modal_schur",
    )(sizes, phi, ck, cm, eigen, sel)
    return k_bb + summed[0], m_bb + summed[1]


def solution(mesh):
    in_specs = (
        P("dom", None, "col"),
        P("dom", None, None, "row"),
        P("dom", None, None, "row"),
        P("dom", "col"),
        P("dom"),
        P("dom", None),
        P("dom", "row", "col"),
        P("dom", "row", "col"),
    )
    out_specs = (P("dom", "row", "col"), P("dom", "row", "col"))
    return jax.shard_map(
        per_device, mesh=mesh, in_specs=in_specs, out_specs=out_specs, check_vma=False
    )
```
